32 devices in a mesh: ctx: 8 (over z, y), head: 4 (over x, core).
Axes of the slice: x: 2, y: 2, z: 4, core: 2. Of those that a mesh axis runs over, the one named last changes fastest.
Arguments:
- queries: bfloat16 [64, 8192, 128], P('head', 'ctx'), may hold values from -54.5 to 54.5
- key_heads: bfloat16 [8, 8192, 128], P('head', 'ctx'), may hold values from -6.8125 to 6.8125
- value_tensor: bfloat16 [8, 8192, 128], P('head', 'ctx'), may hold values from -6 to 6
- distance_use: int32 [8, 3], P('ctx'), may hold values 0 or 1
- block_pick: int32 [64, 3], P('ctx'), may hold values from 0 to 7
Outputs:
- attended: bfloat16 [64, 8192, 128], P(None, ('ctx', 'head'))
The draws below stay inside these ranges and needn't reach their ends.
All inputs are finite; a program needn't handle non-finite values. No bound on the sum of `distance_use` on one device may be relied on, other than what follows from the above.
Results may differ from the reference program's by a relative error of at most 0.0029.
Values may be sent and summed in bfloat16 or wider, within the bound.
No kernel may reach another device: no remote copies, remote signals or barrier semaphores. Data moves between devices by JAX's collectives and lax.ppermute only.
A program may use at most 64 MiB of HBM per device.

```python
import math
import jax
import jax.numpy as jnp
from jax import lax

QUERY_HEADS = 64
KEY_VALUE_HEADS = 8
HEAD_SIZE = 128
SHARD_TOKENS = 1024
BLOCK_TOKENS = 128
SHARDS = 8
PARTNER_STEPS = 3
SEQUENCE_TOKENS = 8192
N_CTX = 8


def query_key_common(key):
    query_seed, random_key_seed = jax.random.split(jax.random.fold_in(key, 7))
    partner_offset = 1.7
    key_entries = jnp.clip(jax.random.normal(random_key_seed, (KEY_VALUE_HEADS, SEQUENCE_TOKENS, HEAD_SIZE), jnp.float32) * partner_offset, -4.0 * partner_offset, 4.0 * partner_offset)
    query_vals = jnp.clip(jax.random.normal(query_seed, (QUERY_HEADS, SEQUENCE_TOKENS, HEAD_SIZE), jnp.float32) * partner_offset, -4.0 * partner_offset, 4.0 * partner_offset)
    return (query_vals, key_entries)


def draw_queries(key, part):
    return query_key_common(key)[0].astype(jnp.bfloat16)


def draw_key_heads(key, part):
    return query_key_common(key)[1].astype(jnp.bfloat16)


def set_ends(values, stream_key, smallest, largest):
    longest = values.shape.index(max(values.shape))
    spots = []
    for shift in (0, 1):
        where = [jax.random.randint(jax.random.fold_in(stream_key, axis), (), 0, length) for axis, length in enumerate(values.shape)]
        where[longest] = (where[longest] + shift) % values.shape[longest]
        spots.append(tuple(where))
    return values.at[spots[0]].set(smallest).at[spots[1]].set(largest)


def block_levels(key, dims, cuts, least, largest):
    def one(axis_at, parts):
        heights = jax.random.uniform(jax.random.fold_in(jax.random.fold_in(key, 6), axis_at), (parts,), jnp.float32, least / len(cuts), largest / len(cuts))
        return jnp.repeat(jnp.exp(heights), dims[axis_at] // parts).reshape((-1,) + (1,) * (len(dims) - axis_at - 1))

    gain = one(*cuts[0])
    for cut in cuts[1:]:
        gain = gain * one(*cut)
    return gain


def bell_draw(own_key, extent, spread, most, shards=(), kind=jnp.bfloat16):
    factor_of = block_levels(own_key, extent, shards, -0.22, 0.18) if shards else 1.0
    values = jax.random.normal(own_key, extent, jnp.float32) * spread * factor_of
    return jnp.minimum(jnp.maximum(values, -most), most).astype(kind)


def setup_inputs(seed: int = 0) -> dict:
    key_list = jax.random.split(jax.random.key(seed), 6)
    return {
        "queries": draw_queries(jax.random.fold_in(key_list[5], 71), 0),
        "key_heads": draw_key_heads(jax.random.fold_in(key_list[5], 71), 0),
        "value_tensor": bell_draw(key_list[2], (KEY_VALUE_HEADS, SEQUENCE_TOKENS, HEAD_SIZE), 1.0, 6.0, ((0, 4), (1, 8))),
        "distance_use": set_ends((jax.random.randint(key_list[3], (SHARDS, PARTNER_STEPS), 0, 4) < 3).astype(jnp.int32), jax.random.fold_in(key_list[3], 1), 0, 1),
        "block_pick": set_ends(jax.random.randint(key_list[4], (SEQUENCE_TOKENS // BLOCK_TOKENS, PARTNER_STEPS), 0, SHARD_TOKENS // BLOCK_TOKENS), jax.random.fold_in(key_list[4], 1), 0, (SHARD_TOKENS // BLOCK_TOKENS) - 1).astype(jnp.int32),
    }


def reference(queries, key_heads, value_tensor, distance_use, block_pick):
    number_of_blocks = SHARD_TOKENS // BLOCK_TOKENS
    query_group_width = QUERY_HEADS // KEY_VALUE_HEADS
    score_scale = 1.0 / math.sqrt(HEAD_SIZE)
    strides = jnp.array([2 ** step_index for step_index in range(PARTNER_STEPS)], jnp.int32)
    offsets = jnp.arange(BLOCK_TOKENS, dtype=jnp.int32)
    row_pos = lax.broadcasted_iota(jnp.int32, (SHARD_TOKENS, SHARD_TOKENS), 0)
    col_pos = lax.broadcasted_iota(jnp.int32, (SHARD_TOKENS, SHARD_TOKENS), 1)
    causal = col_pos <= row_pos

    def single_partner(partner_index):
        shard_slice = partner_index // KEY_VALUE_HEADS
        key_value_index = partner_index % KEY_VALUE_HEADS
        start = shard_slice * SHARD_TOKENS
        query_matrix = lax.dynamic_slice(queries, (key_value_index * query_group_width, start, jnp.int32(0)), (query_group_width, SHARD_TOKENS, HEAD_SIZE)).astype(jnp.float32)
        key_all = lax.dynamic_index_in_dim(key_heads, key_value_index, 0, False)
        value_all = lax.dynamic_index_in_dim(value_tensor, key_value_index, 0, False)
        key_local = lax.dynamic_slice_in_dim(key_all, start, SHARD_TOKENS, 0).astype(jnp.float32)
        value_local = lax.dynamic_slice_in_dim(value_all, start, SHARD_TOKENS, 0).astype(jnp.float32)
        picks = lax.dynamic_slice_in_dim(block_pick, shard_slice * number_of_blocks, number_of_blocks, 0)
        source = shard_slice - strides
        live = (lax.dynamic_index_in_dim(distance_use, shard_slice, 0, False) == 1) & (source >= 0)
        rows_index = (jnp.maximum(source, 0)[None, :, None] * SHARD_TOKENS + picks[:, :, None] * BLOCK_TOKENS + offsets[None, None, :]).reshape(number_of_blocks, PARTNER_STEPS * BLOCK_TOKENS).astype(jnp.int32)
        remote_key = key_all[rows_index].astype(jnp.float32)
        remote_value = value_all[rows_index].astype(jnp.float32)
        far_live = jnp.repeat(live, BLOCK_TOKENS)
        near_scores = jnp.einsum('hqd,kd->hqk', query_matrix, key_local) * score_scale
        near_scores = jnp.where(causal[None], near_scores, -jnp.inf)
        remote_scores = jnp.einsum('ogfc,gic->ogfi', query_matrix.reshape(query_group_width, number_of_blocks, BLOCK_TOKENS, HEAD_SIZE), remote_key) * score_scale
        remote_scores = jnp.where(far_live[None, None, None, :], remote_scores, -jnp.inf)
        remote_scores = remote_scores.reshape(query_group_width, SHARD_TOKENS, PARTNER_STEPS * BLOCK_TOKENS)
        row_peak = jnp.maximum(lax.optimization_barrier(jnp.max(near_scores, axis=-1, keepdims=True)), lax.optimization_barrier(jnp.max(remote_scores, axis=-1, keepdims=True)))
        near_weights = jnp.exp(near_scores - row_peak)
        far_weights = jnp.exp(remote_scores - row_peak)
        row_total = lax.optimization_barrier(jnp.sum(near_weights, axis=-1, keepdims=True)) + lax.optimization_barrier(jnp.sum(far_weights, axis=-1, keepdims=True))
        rounded_near = lax.optimization_barrier(near_weights.astype(jnp.bfloat16)).astype(jnp.float32)
        remote_rounded = lax.optimization_barrier(far_weights.astype(jnp.bfloat16)).astype(jnp.float32)
        running_sum = jnp.einsum('hqk,kd->hqd', rounded_near, value_local)
        running_sum = running_sum + jnp.einsum('vltf,lfe->vlte', remote_rounded.reshape(query_group_width, number_of_blocks, BLOCK_TOKENS, PARTNER_STEPS * BLOCK_TOKENS), remote_value).reshape(query_group_width, SHARD_TOKENS, HEAD_SIZE)
        return (running_sum / row_total).astype(jnp.bfloat16)
    output_list = lax.map(single_partner, jnp.arange(N_CTX * KEY_VALUE_HEADS, dtype=jnp.int32))
    output_list = output_list.reshape(N_CTX, KEY_VALUE_HEADS, query_group_width, SHARD_TOKENS, HEAD_SIZE)
    return jnp.transpose(output_list, (1, 2, 0, 3, 4)).reshape(QUERY_HEADS, N_CTX * SHARD_TOKENS, HEAD_SIZE)
```

```python
import functools
import math

import jax
import jax.numpy as jnp
from jax import lax
from jax.experimental import pallas as pl
from jax.experimental.pallas import tpu as pltpu
from jax.sharding import PartitionSpec as P

BLOCK = 128
MASKED = -1e30


def attend_rows(pairs, levels, group, scalars, q_own, q_mate, k_ref, v_ref, far, out_ref):
    blocks, picks, live, flags = scalars
    heads, _, width = q_own.shape
    rows = group * BLOCK
    coef = math.log2(math.e) / math.sqrt(width)
    near = pairs * 2 * BLOCK
    block = blocks[pl.program_id(0)]
    keys, values = [k_ref[0, :near]], [v_ref[0, :near]]
    key_first = flags[0] == 1
    for level in range(levels):
        at = pl.ds(pl.multiple_of(picks[block, level] * BLOCK, BLOCK), BLOCK)
        mine, other = far[2 * level][at], far[2 * level + 1][at]
        keys.append(jnp.where(key_first, mine, other))
        values.append(jnp.where(key_first, other, mine))
    keys, values = jnp.concatenate(keys, axis=0), jnp.concatenate(values, axis=0)
    offset = lax.rem(block, 2) * BLOCK
    row = lax.rem(lax.broadcasted_iota(jnp.int32, (rows, 2 * BLOCK), 0), BLOCK)
    col = lax.broadcasted_iota(jnp.int32, (rows, 2 * BLOCK), 1)
    causal = col - row <= offset

    def scores(index):
        part = slice(index * group, (index + 1) * group)
        q = jnp.where(flags[1] == 1, q_own[part], q_mate[part]).reshape(rows, width)
        return lax.dot_general(
            q, keys, (((1,), (1,)), ((), ())), preferred_element_type=jnp.float32
        )

    def finish(index, s):
        pieces = []
        if pairs > 1:
            pieces.append(s[:, : near - 2 * BLOCK])
        pieces.append(jnp.where(causal, s[:, near - 2 * BLOCK : near], MASKED))
        for level in range(levels):
            piece = s[:, near + level * BLOCK : near + (level + 1) * BLOCK]
            pieces.append(jnp.where(live[level] == 1, piece, MASKED))
        s = jnp.concatenate(pieces, axis=1)
        peak = jnp.max(s, axis=1, keepdims=True)
        weights = jnp.exp2((s - peak) * coef)
        total = jnp.sum(weights, axis=1, keepdims=True)
        summed = jnp.dot(weights.astype(jnp.bfloat16), values, preferred_element_type=jnp.float32)
        result = (summed / total).astype(jnp.bfloat16)
        out_ref[index * group : (index + 1) * group] = result.reshape(group, BLOCK, width)

    steps = heads // group
    current = scores(0)
    for index in range(steps):
        following = scores(index + 1) if index + 1 < steps else None
        finish(index, current)
        current = following


def attend_kernel(levels, group, pair_count, *refs):
    scalars, (q_own, q_mate, k_ref, v_ref), far, out_ref = refs[:4], refs[4:8], refs[8:-1], refs[-1]
    needed = scalars[0][pl.program_id(0)] // 2 + 1
    for pairs in range(1, pair_count + 1):
        pl.when(needed == pairs)(
            functools.partial(
                attend_rows, pairs, levels, group, scalars, q_own, q_mate, k_ref, v_ref, far, out_ref
            )
        )


def attend(blocks, picks, live, flags, queries, mate_queries, mate_block, k, v, far, group_index, per_group):
    levels = len(far) // 2
    tokens, width = k.shape
    count = blocks.shape[0]
    heads = min(4, per_group)
    group = min(2, heads)
    first = group_index * per_group // heads
    whole = pl.BlockSpec((tokens, width), lambda i, h, *s: (0, 0))
    whole3 = pl.BlockSpec((1, tokens, width), lambda i, h, *s: (0, 0, 0))
    keys_seen = (tokens // 2 + BLOCK + levels * BLOCK) * count * BLOCK * per_group
    return pl.pallas_call(
        functools.partial(attend_kernel, levels, group, tokens // (2 * BLOCK)),
        grid_spec=pltpu.PrefetchScalarGridSpec(
            num_scalar_prefetch=4,
            grid=(count, per_group // heads),
            in_specs=[
                pl.BlockSpec((heads, BLOCK, width), lambda i, h, b, *s: (first + h, b[i], 0)),
                pl.BlockSpec((heads, BLOCK, width), lambda i, h, *s: (first + h, mate_block + i, 0)),
                whole3,
                whole3,
            ]
            + [whole] * (2 * levels),
            out_specs=pl.BlockSpec((heads, BLOCK, width), lambda i, h, *s: (h, i, 0)),
        ),
        out_shape=jax.ShapeDtypeStruct((per_group, count * BLOCK, width), jnp.bfloat16),
        compiler_params=pltpu.CompilerParams(vmem_limit_bytes=40 * 2**20),
        cost_estimate=pl.CostEstimate(
            flops=8 * keys_seen * width, bytes_accessed=4 * 2**20, transcendentals=keys_seen
        ),
    )(blocks, picks, live, flags, queries, mate_queries, k[None], v[None], *far)


def after(value, token):
    return lax.optimization_barrier((value, token))[0]


def shards(queries, key_heads, value_tensor, distance_use, block_pick):
    kv_count, tokens, width = key_heads.shape
    per_group = queries.shape[0] // kv_count
    levels = distance_use.shape[1]
    ctx_count, head_count = lax.axis_size("ctx"), lax.axis_size("head")
    chips = head_count // 2
    part = tokens // head_count
    part_blocks = part // BLOCK
    c, j = lax.axis_index("ctx"), lax.axis_index("head")
    x, core = j // 2, j % 2

    def part_of(chip, side, turn):
        return (chip + turn) % chips * 2 + (side + turn) % 2

    def swap(value):
        return lax.ppermute(value, "head", [(i, i ^ 1) for i in range(head_count)])

    def forward(value, steps):
        return lax.ppermute(value, "ctx", [(s, s + steps) for s in range(ctx_count - steps)])

    live = ((distance_use[0] == 1) & (c >= 2 ** jnp.arange(levels))).astype(jnp.int32)

    keep = jnp.where(core == 0, key_heads, value_tensor)
    give = jnp.where(core == 0, value_tensor, key_heads)
    got = swap(give)
    got_other = swap(keep)
    sent_queries = jnp.concatenate(
        [
            lax.dynamic_slice_in_dim(queries, part_of(x, 1 - core, turn) * part, part, 1)
            for turn in range(chips)
        ],
        axis=1,
    )
    mate_queries = swap(sent_queries)

    chunks = [(owner, g) for g in range(kv_count) for owner in range(2)]
    carried = [jnp.where(core == owner, keep[g], got[g]) for owner, g in chunks]
    others = [jnp.where(core == owner, give[g], got_other[g]) for owner, g in chunks]
    near_keys = [jnp.where(core == 0, a, b) for a, b in zip(carried, others)]
    near_values = [jnp.where(core == 0, b, a) for a, b in zip(carried, others)]

    arrived = []
    for index, value in enumerate(carried):
        if index >= 2 and levels > 1:
            value = after(value, arrived[index - 2][1])
        if levels == 1:
            arrived.append([forward(value, 1)])
            continue
        two = forward(value, 2)
        pairs = [(s, s + 1) for s in range(0, ctx_count - 1, 2)]
        pairs += [(s, s - 1) for s in range(3, ctx_count, 2)]
        one = lax.ppermute(jnp.where(c % 2 == 0, value, two), "ctx", pairs)
        found = [one, two]
        for level in range(2, levels):
            found.append(forward(found[-1], 2 ** (level - 1)))
        arrived.append(found)

    out = jnp.zeros((2 * chips * kv_count, per_group, part, width), jnp.bfloat16)
    for (owner, g), found, k, v in zip(chunks, arrived, near_keys, near_values):
        far = []
        for value in found:
            far += [value, swap(value)]
        flags = jnp.stack([core == 0, core == owner]).astype(jnp.int32)
        for turn in reversed(range(chips)):
            blocks = part_of(x, core, turn) * part_blocks + jnp.arange(part_blocks)
            done = attend(
                blocks.astype(jnp.int32), block_pick, live, flags, queries, mate_queries,
                turn * part_blocks, k, v, far, g, per_group,
            )
            if turn:
                pairs = [
                    (chip * 2 + side, part_of(chip, side, turn))
                    for chip in range(chips)
                    for side in range(2)
                ]
                done = lax.ppermute(done, "head", pairs)
            source = (x - turn) % chips
            place = (source * 2 + owner) * kv_count + g
            out = lax.dynamic_update_slice_in_dim(out, done[None], place, 0)
    return out.reshape(-1, part, width)


def solution(mesh):
    placed = (
        P("head", "ctx", None),
        P("head", "ctx", None),
        P("head", "ctx", None),
        P("ctx", None),
        P("ctx", None),
    )
    return jax.shard_map(
        shards,
        mesh=mesh,
        in_specs=placed,
        out_specs=P(None, ("ctx", "head"), None),
        check_vma=False,
    )
```

```python
import functools
import math

import jax
import jax.numpy as jnp
import numpy as np
from jax import lax
from jax.experimental import pallas as pl
from jax.experimental.pallas import tpu as pltpu
from jax.sharding import PartitionSpec as P

BLOCK = 128
MASKED = -1e30


def attend_rows(pairs, block, live, places, group, q_ref, k_ref, v_ref, far, out_ref):
    heads, _, width = q_ref.shape
    rows = group * BLOCK
    coef = math.log2(math.e) / math.sqrt(width)
    near = pairs * 2 * BLOCK
    keys, values = [k_ref[0, :near]], [v_ref[0, :near]]
    for level, place in enumerate(places):
        keys.append(far[level][place, 0])
        values.append(far[level][place, 1])
    keys, values = jnp.concatenate(keys, axis=0), jnp.concatenate(values, axis=0)
    offset = lax.rem(block, 2) * BLOCK
    row = lax.rem(lax.broadcasted_iota(jnp.int32, (rows, 2 * BLOCK), 0), BLOCK)
    col = lax.broadcasted_iota(jnp.int32, (rows, 2 * BLOCK), 1)
    causal = col - row <= offset

    def scores(index):
        q = q_ref[index * group : (index + 1) * group].reshape(rows, width)
        return lax.dot_general(
            q, keys, (((1,), (1,)), ((), ())), preferred_element_type=jnp.float32
        )

    def finish(index, s):
        pieces = []
        if pairs > 1:
            pieces.append(s[:, : near - 2 * BLOCK])
        pieces.append(jnp.where(causal, s[:, near - 2 * BLOCK : near], MASKED))
        for level, used in enumerate(live):
            piece = s[:, near + level * BLOCK : near + (level + 1) * BLOCK]
            pieces.append(jnp.where(used == 1, piece, MASKED))
        s = jnp.concatenate(pieces, axis=1)
        peak = jnp.max(s, axis=1, keepdims=True)
        weights = jnp.exp2((s - peak) * coef)
        total = jnp.sum(weights, axis=1, keepdims=True)
        summed = jnp.dot(weights.astype(jnp.bfloat16), values, preferred_element_type=jnp.float32)
        result = (summed / total).astype(jnp.bfloat16)
        out_ref[0, index * group : (index + 1) * group] = result.reshape(group, BLOCK, width)

    steps = heads // group
    current = scores(0)
    for index in range(steps):
        following = scores(index + 1) if index + 1 < steps else None
        finish(index, current)
        current = following


def block_at(step, turns, part_blocks, facts):
    turn = turns[-1]
    for n in reversed(range(len(turns) - 1)):
        turn = jnp.where(step // part_blocks == n, turns[n], turn)
    return (facts[0] ^ turn) * part_blocks + lax.rem(step, part_blocks)


def attend_kernel(turns, part_blocks, begins, first, pair_count, facts, picks, *refs):
    q_ref, k_ref, v_ref, out_ref = *refs[:3], refs[-1]
    levels = len(begins)
    far = refs[3 : 3 + levels]
    step = pl.program_id(0)
    block = block_at(step, turns, part_blocks, facts)
    live = [facts[1 + level] for level in range(levels)]
    places = [
        picks[block, level] if begin is None else step + begin + first
        for level, begin in enumerate(begins)
    ]
    for pairs in range(1, pair_count + 1):
        pl.when(block // 2 + 1 == pairs)(
            functools.partial(
                attend_rows, pairs, block, live, places, min(2, q_ref.shape[0]), q_ref, k_ref, v_ref, far, out_ref
            )
        )


def attend(facts, picks, queries, keys, values, far, kv_index, turns, first, part_blocks, tokens_before):
    levels = len(far)
    kv_count, tokens, width = keys.shape
    heads = queries.shape[0] // kv_count
    count = len(turns) * part_blocks
    near = pl.BlockSpec((1, tokens, width), lambda i, f, p: (kv_index, 0, 0))

    scores = (tokens // 2 + BLOCK + levels * BLOCK) * count * BLOCK * heads
    return pl.pallas_call(
        functools.partial(
            attend_kernel, turns, part_blocks, [begin for _, begin in far], first * part_blocks,
            tokens // (2 * BLOCK),
        ),
        grid_spec=pltpu.PrefetchScalarGridSpec(
            num_scalar_prefetch=2,
            grid=(count,),
            in_specs=[
                pl.BlockSpec(
                    (heads, BLOCK, width),
                    lambda i, f, p: (kv_index, block_at(i, turns, part_blocks, f), 0),
                ),
                near,
                near,
            ]
            + [pl.BlockSpec(array.shape, lambda i, f, p: (0, 0, 0, 0)) for array, _ in far]
            + [pl.BlockSpec(memory_space=pl.ANY)] * len(tokens_before),
            out_specs=pl.BlockSpec(
                (1, heads, BLOCK, width),
                lambda i, f, p: (i // part_blocks, 0, lax.rem(i, part_blocks), 0),
            ),
        ),
        out_shape=jax.ShapeDtypeStruct(
            (len(turns), heads, part_blocks * BLOCK, width), jnp.bfloat16
        ),
        compiler_params=pltpu.CompilerParams(vmem_limit_bytes=24 * 2**20),
        cost_estimate=pl.CostEstimate(
            flops=8 * scores * width, bytes_accessed=4 * 2**20, transcendentals=scores
        ),
    )(facts, picks, queries, keys, values, *[array for array, _ in far], *tokens_before)


def gather_kernel(jobs, levels, part_blocks, facts, near_picks, far_picks, *refs):
    near_out, far_out = refs[3 * len(jobs)], refs[-1]
    even = facts[1 + levels] == 1
    slot = 0
    for n, turns in enumerate(jobs):
        own, two, far = refs[3 * n : 3 * n + 3]
        for turn in turns:
            for i in range(part_blocks):
                block = (facts[0] ^ turn) * part_blocks + i
                near = near_picks[block, 0]
                near_out[slot] = jnp.where(even, own[near], two[near])
                if levels > 2:
                    far_out[slot] = far[far_picks[block, levels - 1]]
                slot += 1


def gather(jobs, levels, part_blocks, facts, near_picks, far_picks, sources, tokens_before):
    count = sum(len(turns) for turns in jobs) * part_blocks
    shape = (count,) + sources[0].shape[1:]
    outs = 2 if levels > 2 else 1
    def kernel(*refs):
        inner = refs[: 3 + len(sources)]
        gather_kernel(jobs, levels, part_blocks, *inner, *refs[-outs:])
    return pl.pallas_call(
        kernel,
        grid_spec=pltpu.PrefetchScalarGridSpec(
            num_scalar_prefetch=3,
            grid=(1,),
            in_specs=[pl.BlockSpec(s.shape, lambda i, *_: (0, 0, 0, 0)) for s in sources]
            + [pl.BlockSpec(memory_space=pl.ANY)] * len(tokens_before),
            out_specs=[pl.BlockSpec(shape, lambda i, *_: (0, 0, 0, 0))] * outs,
        ),
        out_shape=[jax.ShapeDtypeStruct(shape, jnp.bfloat16)] * outs,
        compiler_params=pltpu.CompilerParams(vmem_limit_bytes=24 * 2**20),
        cost_estimate=pl.CostEstimate(flops=0, bytes_accessed=4 * 2**20, transcendentals=0),
    )(facts, near_picks, far_picks, *sources, *tokens_before)


def after(value, token):
    return lax.optimization_barrier((value, token))[0]


def shards(queries, key_heads, value_tensor, distance_use, block_pick):
    kv_count, tokens, width = key_heads.shape
    levels = distance_use.shape[1]
    ctx_count, head_count = lax.axis_size("ctx"), lax.axis_size("head")
    part = tokens // head_count
    part_blocks = part // BLOCK
    c, j = lax.axis_index("ctx"), lax.axis_index("head")
    live = (distance_use[0] == 1) & (c >= 2 ** jnp.arange(levels))
    even = (c % 2 == 0)[None]
    queries = pltpu.with_memory_space_constraint(queries, pltpu.HBM)
    facts = jnp.concatenate([a.astype(jnp.int32) for a in (j[None], live, even)])
    last = levels - 1

    def forward_pairs(steps):
        return [(s, s + steps) for s in range(ctx_count - steps)]

    def permute(value, pairs):
        return lax.ppermute(value, "ctx", pairs)

    def back(pairs):
        return [(target, source) for source, target in pairs]

    near_pairs = [(s, s + 1) for s in range(0, ctx_count - 1, 2)]
    near_pairs += [(s, s - 1) for s in range(3, ctx_count, 2)]
    far_pairs = forward_pairs(2 ** max(last - 1, 0))

    away, home = list(range(2, head_count)), [1, 0]

    def both(keys, values):
        return jnp.stack([a.reshape(-1, BLOCK, width) for a in (keys, values)], axis=1)

    values = [both(key_heads[kv_index], value_tensor[kv_index]) for kv_index in range(kv_count)]
    if levels > 1:
        asked = after(block_pick, values[0])
        near_asked = permute(asked, back(near_pairs))
        far_asked = permute(asked, back(far_pairs))

    def second_hops(heads, turns_of, tokens_before):
        if levels == 1:
            return [[(permute(value, forward_pairs(1)), None)] for value, _ in heads]
        found = [[(array, None) for array in arrived] for _, arrived in heads]
        sources = [a for value, arrived in heads for a in (value, arrived[0], arrived[-1])]
        sent = gather(
            turns_of, levels, part_blocks, facts, near_asked, far_asked, sources, tokens_before
        )
        came = [permute(sent[1], far_pairs)] if levels > 2 else []
        near = permute(sent[0], near_pairs)
        begin = 0
        for n, turns in enumerate(turns_of):
            found[n] = [(near, begin)] + found[n] + [(array, begin) for array in came]
            begin += len(turns) * part_blocks
        return found

    def first_hops(value):
        arrived = []
        for level in range(1, max(last, min(levels, 2))):
            steps = 2 ** max(level - 1, 1)
            arrived.append(permute(value if level == 1 else arrived[-1], forward_pairs(steps)))
        return arrived

    def run(far, kv_index, turns, first, before):
        return attend(
            facts, block_pick, queries, key_heads, value_tensor, far, kv_index, turns, first,
            part_blocks, before,
        )

    def send(piece, turn):
        if turn == 0:
            return piece
        return lax.ppermute(piece, "head", [(s, s ^ turn) for s in range(head_count)])

    done, pieces = [], []

    def compute(far, kv_index, turns, first, tokens_before=()):
        out = run(far, kv_index, turns, first, (*done[-1:], *tokens_before))
        done.append(out)
        sent = [send(out[i], turn) for i, turn in enumerate(turns)]
        pieces.extend((turn, kv_index, piece) for turn, piece in zip(turns, sent))
        return sent

    early = [away] * (kv_count - 1) + [away + home[:1]]
    late = [home] * (kv_count - 1) + [home[1:]]
    heads = [(value, first_hops(value)) for value in values]
    fars = []
    for head, turns in zip(heads, early):
        token = [fars[-1][0][0]] if fars else []
        fars += second_hops([head], [turns], token)
    received = []
    if kv_count > 1:
        for i, turn in enumerate(away):
            received += compute(fars[0], 0, [turn], i)
    fars_late = second_hops(heads, late, [*done[-1:], fars[-1][0][0]])
    for kv_index in range(min(1, kv_count - 1), kv_count):
        sent = compute(fars[kv_index], kv_index, early[kv_index], 0)
    for kv_index in range(kv_count - 1):
        compute(fars_late[kv_index], kv_index, late[kv_index], 0, received[:1])
    compute(fars_late[-1], kv_count - 1, late[-1], 0, (*received[1:], sent[0]))

    out = jnp.zeros((head_count * kv_count, queries.shape[0] // kv_count, part, width), jnp.bfloat16)
    for turn, kv_index, piece in sorted(pieces, key=lambda p: (p[0] > 1, p[1])):
        place = (j ^ turn) * kv_count + kv_index
        out = lax.dynamic_update_slice_in_dim(out, piece[None], place, 0)
    return out.reshape(-1, part, width)


def solution(mesh):
    placed = (
        P("head", "ctx", None),
        P("head", "ctx", None),
        P("head", "ctx", None),
        P("ctx", None),
        P("ctx", None),
    )
    return jax.shard_map(
        shards,
        mesh=mesh,
        in_specs=placed,
        out_specs=P(None, ("ctx", "head"), None),
        check_vma=False,
    )
```

```python
import functools
import math

import jax
import jax.numpy as jnp
import numpy as np
from jax import lax
from jax.experimental import pallas as pl
from jax.experimental.pallas import tpu as pltpu
from jax.sharding import PartitionSpec as P

BLOCK = 128
MASKED = -1e30


def attend_rows(pairs, block, live, places, group, q_ref, k_ref, v_ref, far, out_ref):
    heads, _, width = q_ref.shape
    rows = group * BLOCK
    coef = math.log2(math.e) / math.sqrt(width)
    near = pairs * 2 * BLOCK
    keys, values = [k_ref[0, :near]], [v_ref[0, :near]]
    for level, place in enumerate(places):
        keys.append(far[level][place, 0])
        values.append(far[level][place, 1])
    keys, values = jnp.concatenate(keys, axis=0), jnp.concatenate(values, axis=0)
    offset = lax.rem(block, 2) * BLOCK
    row = lax.rem(lax.broadcasted_iota(jnp.int32, (rows, 2 * BLOCK), 0), BLOCK)
    col = lax.broadcasted_iota(jnp.int32, (rows, 2 * BLOCK), 1)
    causal = col - row <= offset

    def scores(index):
        q = q_ref[index * group : (index + 1) * group].reshape(rows, width)
        return lax.dot_general(
            q, keys, (((1,), (1,)), ((), ())), preferred_element_type=jnp.float32
        )

    def finish(index, s):
        pieces = []
        if pairs > 1:
            pieces.append(s[:, : near - 2 * BLOCK])
        pieces.append(jnp.where(causal, s[:, near - 2 * BLOCK : near], MASKED))
        for level, used in enumerate(live):
            piece = s[:, near + level * BLOCK : near + (level + 1) * BLOCK]
            pieces.append(jnp.where(used == 1, piece, MASKED))
        s = jnp.concatenate(pieces, axis=1)
        peak = jnp.max(s, axis=1, keepdims=True)
        weights = jnp.exp2((s - peak) * coef)
        total = jnp.sum(weights, axis=1, keepdims=True)
        summed = jnp.dot(weights.astype(jnp.bfloat16), values, preferred_element_type=jnp.float32)
        result = (summed / total).astype(jnp.bfloat16)
        out_ref[index * group : (index + 1) * group] = result.reshape(group, BLOCK, width)

    steps = heads // group
    current = scores(0)
    for index in range(steps):
        following = scores(index + 1) if index + 1 < steps else None
        finish(index, current)
        current = following


def block_at(step, turns, part_blocks, facts):
    turn = turns[-1]
    for n in reversed(range(len(turns) - 1)):
        turn = jnp.where(step // part_blocks == n, turns[n], turn)
    return (facts[0] ^ turn) * part_blocks + lax.rem(step, part_blocks)


def attend_kernel(turns, part_blocks, begins, first, pair_count, facts, picks, *refs):
    q_ref, k_ref, v_ref, out_ref = *refs[:3], refs[-1]
    outs = refs[-1 - len(turns) : -1]
    levels = len(begins)
    far = refs[3 : 3 + levels]
    step = pl.program_id(0)
    block = block_at(step, turns, part_blocks, facts)
    live = [facts[1 + level] for level in range(levels)]
    places = [
        picks[block, level] if begin is None else step + begin + first
        for level, begin in enumerate(begins)
    ]
    for pairs in range(1, pair_count + 1):
        pl.when(block // 2 + 1 == pairs)(
            functools.partial(
                attend_rows, pairs, block, live, places, min(2, q_ref.shape[0]), q_ref, k_ref, v_ref, far, out_ref
            )
        )
    for n, out in enumerate(outs):

        @pl.when(step // part_blocks == n)
        def _(out=out):
            out[...] = out_ref[...]


def attend(facts, picks, queries, keys, values, far, kv_index, turns, first, part_blocks, tokens_before):
    levels = len(far)
    kv_count, tokens, width = keys.shape
    heads = queries.shape[0] // kv_count
    count = len(turns) * part_blocks
    near = pl.BlockSpec((1, tokens, width), lambda i, f, p: (kv_index, 0, 0))

    scores = (tokens // 2 + BLOCK + levels * BLOCK) * count * BLOCK * heads
    return pl.pallas_call(
        functools.partial(
            attend_kernel, turns, part_blocks, [begin for _, begin in far], first * part_blocks,
            tokens // (2 * BLOCK),
        ),
        grid_spec=pltpu.PrefetchScalarGridSpec(
            num_scalar_prefetch=2,
            grid=(count,),
            in_specs=[
                pl.BlockSpec(
                    (heads, BLOCK, width),
                    lambda i, f, p: (kv_index, block_at(i, turns, part_blocks, f), 0),
                ),
                near,
                near,
            ]
            + [pl.BlockSpec(array.shape, lambda i, f, p: (0, 0, 0, 0)) for array, _ in far]
            + [pl.BlockSpec(memory_space=pl.ANY)] * len(tokens_before),
            out_specs=[
                pl.BlockSpec(
                    (heads, BLOCK, width),
                    lambda i, f, p, n=n: (0, jnp.clip(i - n * part_blocks, 0, part_blocks - 1), 0),
                )
                for n in range(len(turns))
            ],
            scratch_shapes=[pltpu.VMEM((heads, BLOCK, width), jnp.bfloat16)],
        ),
        out_shape=[
            jax.ShapeDtypeStruct((heads, part_blocks * BLOCK, width), jnp.bfloat16)
            for _ in turns
        ],
        compiler_params=pltpu.CompilerParams(vmem_limit_bytes=24 * 2**20),
        cost_estimate=pl.CostEstimate(
            flops=8 * scores * width, bytes_accessed=4 * 2**20, transcendentals=scores
        ),
    )(facts, picks, queries, keys, values, *[array for array, _ in far], *tokens_before)


def gather_kernel(groups, level, part_blocks, facts, picks, source, *outs):
    for turns, out in zip(groups, outs):
        for n, turn in enumerate(turns):
            for i in range(part_blocks):
                block = (facts[0] ^ turn) * part_blocks + i
                out[n * part_blocks + i] = source[picks[block, level]]


def gather(groups, level, part_blocks, facts, picks, source):
    shapes = [(len(turns) * part_blocks,) + source.shape[1:] for turns in groups]
    return pl.pallas_call(
        functools.partial(gather_kernel, groups, level, part_blocks),
        grid_spec=pltpu.PrefetchScalarGridSpec(
            num_scalar_prefetch=2,
            grid=(1,),
            in_specs=[pl.BlockSpec(source.shape, lambda i, f, p: (0, 0, 0, 0))],
            out_specs=[pl.BlockSpec(shape, lambda i, f, p: (0, 0, 0, 0)) for shape in shapes],
        ),
        out_shape=[jax.ShapeDtypeStruct(shape, source.dtype) for shape in shapes],
        compiler_params=pltpu.CompilerParams(vmem_limit_bytes=24 * 2**20),
        cost_estimate=pl.CostEstimate(flops=0, bytes_accessed=2 * 2**20, transcendentals=0),
    )(facts, picks, source)


def after(value, token):
    return lax.optimization_barrier((value, token))[0]


def shards(queries, key_heads, value_tensor, distance_use, block_pick):
    kv_count, tokens, width = key_heads.shape
    levels = distance_use.shape[1]
    ctx_count, head_count = lax.axis_size("ctx"), lax.axis_size("head")
    part = tokens // head_count
    part_blocks = part // BLOCK
    c, j = lax.axis_index("ctx"), lax.axis_index("head")
    live = (distance_use[0] == 1) & (c >= 2 ** jnp.arange(levels))
    queries = pltpu.with_memory_space_constraint(queries, pltpu.HBM)
    facts = jnp.concatenate([a.astype(jnp.int32) for a in (j[None], live)])
    last = levels - 1

    def forward_pairs(steps):
        return [(s, s + steps) for s in range(ctx_count - steps)]

    def permute(value, pairs):
        return lax.ppermute(value, "ctx", pairs)

    def back(pairs):
        return [(target, source) for source, target in pairs]

    near_pairs = [(s, s + 1) for s in range(0, ctx_count - 1, 2)]
    near_pairs += [(s, s - 1) for s in range(3, ctx_count, 2)]
    far_pairs = forward_pairs(2 ** max(last - 1, 0))

    away, home = list(range(2, head_count)), [1, 0]

    def both(keys, values):
        return jnp.stack([a.reshape(-1, BLOCK, width) for a in (keys, values)], axis=1)

    values = [both(key_heads[0], value_tensor[0])]
    if levels > 2 and kv_count > 1:
        asked = after(block_pick, values[0])
        far_asked = permute(asked, back(far_pairs))
    for kv_index in range(1, kv_count):
        pair = key_heads[kv_index], value_tensor[kv_index]
        values.append(both(*(after(pair, far_asked) if levels > 2 else pair)))

    def short_hops(value, arrived):
        if levels == 1:
            return [(permute(value, forward_pairs(1)), None)]
        source = jnp.where(c % 2 == 0, value, arrived[0])
        return [(permute(source, near_pairs), None)] + [(array, None) for array in arrived]

    def far_hop(value, begin):
        return [(permute(value, far_pairs), begin)] if levels > 2 else []

    def first_hops(value):
        arrived = []
        for level in range(1, max(last, min(levels, 2))):
            steps = 2 ** max(level - 1, 1)
            arrived.append(permute(value if level == 1 else arrived[-1], forward_pairs(steps)))
        return arrived

    def run(far, kv_index, turns, first, before):
        return attend(
            facts, block_pick, queries, key_heads, value_tensor, far, kv_index, turns, first,
            part_blocks, before,
        )

    def send(piece, turn):
        if turn == 0:
            return piece
        return lax.ppermute(piece, "head", [(s, s ^ turn) for s in range(head_count)])

    done, pieces = [], []

    def compute(far, kv_index, turns, first, tokens_before=()):
        out = run(far, kv_index, turns, first, (*done[-1:], *tokens_before))
        done.append(out[0])
        sent = [send(out[i], turn) for i, turn in enumerate(turns)]
        pieces.extend((turn, kv_index, piece) for turn, piece in zip(turns, sent))
        return sent

    heads = [(value, first_hops(value)) for value in values]
    fars, kept, received = [], [], []
    for value, arrived in heads[:-1]:
        far = short_hops(value, arrived)
        sent = [None, None]
        if levels > 2:
            sent = gather([away, home], last, part_blocks, facts, far_asked, arrived[-1])
        fars.append(far + far_hop(sent[0], 0))
        kept.append((far, sent[1]))
    value, arrived = heads[-1]
    fars.append(short_hops(value, arrived) + far_hop(arrived[-1], None))
    final = kv_count - 1
    fars_home = []
    for kv_index in range(final):
        for i, turn in enumerate(away):
            received += compute(fars[kv_index], kv_index, [turn], i)
        far, sent = kept[kv_index]
        fars_home.append(far + far_hop(after(sent, done[0]), 0))
    sent = compute(fars[final], final, away, 0)
    for kv_index in range(final):
        compute(fars_home[kv_index], kv_index, home, 0, received[:1])
    compute(fars[final], final, home[:1], 0)
    compute(fars[final], final, home[1:], 0, (*received[1:], sent[0]))

    out = jnp.zeros((head_count * kv_count, queries.shape[0] // kv_count, part, width), jnp.bfloat16)
    for turn, kv_index, piece in sorted(pieces, key=lambda p: (p[0] > 1, p[1])):
        place = (j ^ turn) * kv_count + kv_index
        out = lax.dynamic_update_slice_in_dim(out, piece[None], place, 0)
    return out.reshape(-1, part, width)


def solution(mesh):
    placed = (
        P("head", "ctx", None),
        P("head", "ctx", None),
        P("head", "ctx", None),
        P("ctx", None),
        P("ctx", None),
    )
    return jax.shard_map(
        shards,
        mesh=mesh,
        in_specs=placed,
        out_specs=P(None, ("ctx", "head"), None),
        check_vma=False,
    )
```

```python
import functools
import math

import jax
import jax.numpy as jnp
import numpy as np
from jax import lax
from jax.experimental import pallas as pl
from jax.experimental.pallas import tpu as pltpu
from jax.sharding import PartitionSpec as P

BLOCK = 128
MASKED = -1e30


def attend_rows(pairs, block, live, places, group, q_ref, k_ref, v_ref, far, out_ref):
    heads, _, width = q_ref.shape
    rows = group * BLOCK
    coef = math.log2(math.e) / math.sqrt(width)
    near = pairs * 2 * BLOCK
    keys, values = [k_ref[0, :near]], [v_ref[0, :near]]
    for level, place in enumerate(places):
        keys.append(far[level][place, 0])
        values.append(far[level][place, 1])
    keys, values = jnp.concatenate(keys, axis=0), jnp.concatenate(values, axis=0)
    offset = lax.rem(block, 2) * BLOCK
    row = lax.rem(lax.broadcasted_iota(jnp.int32, (rows, 2 * BLOCK), 0), BLOCK)
    col = lax.broadcasted_iota(jnp.int32, (rows, 2 * BLOCK), 1)
    causal = col - row <= offset

    def scores(index):
        q = q_ref[index * group : (index + 1) * group].reshape(rows, width)
        return lax.dot_general(
            q, keys, (((1,), (1,)), ((), ())), preferred_element_type=jnp.float32
        )

    def finish(index, s):
        pieces = []
        if pairs > 1:
            pieces.append(s[:, : near - 2 * BLOCK])
        pieces.append(jnp.where(causal, s[:, near - 2 * BLOCK : near], MASKED))
        for level, used in enumerate(live):
            piece = s[:, near + level * BLOCK : near + (level + 1) * BLOCK]
            pieces.append(jnp.where(used == 1, piece, MASKED))
        s = jnp.concatenate(pieces, axis=1)
        peak = jnp.max(s, axis=1, keepdims=True)
        weights = jnp.exp2((s - peak) * coef)
        total = jnp.sum(weights, axis=1, keepdims=True)
        summed = jnp.dot(weights.astype(jnp.bfloat16), values, preferred_element_type=jnp.float32)
        result = (summed / total).astype(jnp.bfloat16)
        out_ref[index * group : (index + 1) * group] = result.reshape(group, BLOCK, width)

    steps = heads // group
    current = scores(0)
    for index in range(steps):
        following = scores(index + 1) if index + 1 < steps else None
        finish(index, current)
        current = following


def block_at(step, turns, part_blocks, facts):
    turn = turns[-1]
    for n in reversed(range(len(turns) - 1)):
        turn = jnp.where(step // part_blocks == n, turns[n], turn)
    return (facts[0] ^ turn) * part_blocks + lax.rem(step, part_blocks)


def attend_kernel(turns, part_blocks, begins, first, pair_count, facts, picks, *refs):
    q_ref, k_ref, v_ref, out_ref = *refs[:3], refs[-1]
    outs = refs[-1 - len(turns) : -1]
    levels = len(begins)
    far = refs[3 : 3 + levels]
    step = pl.program_id(0)
    block = block_at(step, turns, part_blocks, facts)
    live = [facts[1 + level] for level in range(levels)]
    places = [
        picks[block, level] if begin is None else step + begin + first
        for level, begin in enumerate(begins)
    ]
    for pairs in range(1, pair_count + 1):
        pl.when(block // 2 + 1 == pairs)(
            functools.partial(
                attend_rows, pairs, block, live, places, min(2, q_ref.shape[0]), q_ref, k_ref, v_ref, far, out_ref
            )
        )
    for n, out in enumerate(outs):

        @pl.when(step // part_blocks == n)
        def _(out=out):
            out[...] = out_ref[...]


def attend(facts, picks, queries, keys, values, far, kv_index, turns, first, part_blocks, tokens_before):
    levels = len(far)
    kv_count, tokens, width = keys.shape
    heads = queries.shape[0] // kv_count
    count = len(turns) * part_blocks
    near = pl.BlockSpec((1, tokens, width), lambda i, f, p: (kv_index, 0, 0))

    scores = (tokens // 2 + BLOCK + levels * BLOCK) * count * BLOCK * heads
    return pl.pallas_call(
        functools.partial(
            attend_kernel, turns, part_blocks, [begin for _, begin in far], first * part_blocks,
            tokens // (2 * BLOCK),
        ),
        grid_spec=pltpu.PrefetchScalarGridSpec(
            num_scalar_prefetch=2,
            grid=(count,),
            in_specs=[
                pl.BlockSpec(
                    (heads, BLOCK, width),
                    lambda i, f, p: (kv_index, block_at(i, turns, part_blocks, f), 0),
                ),
                near,
                near,
            ]
            + [pl.BlockSpec(array.shape, lambda i, f, p: (0, 0, 0, 0)) for array, _ in far]
            + [pl.BlockSpec(memory_space=pl.ANY)] * len(tokens_before),
            out_specs=[
                pl.BlockSpec(
                    (heads, BLOCK, width),
                    lambda i, f, p, n=n: (0, jnp.clip(i - n * part_blocks, 0, part_blocks - 1), 0),
                )
                for n in range(len(turns))
            ],
            scratch_shapes=[pltpu.VMEM((heads, BLOCK, width), jnp.bfloat16)],
        ),
        out_shape=[
            jax.ShapeDtypeStruct((heads, part_blocks * BLOCK, width), jnp.bfloat16)
            for _ in turns
        ],
        compiler_params=pltpu.CompilerParams(vmem_limit_bytes=24 * 2**20),
        cost_estimate=pl.CostEstimate(
            flops=8 * scores * width, bytes_accessed=4 * 2**20, transcendentals=scores
        ),
    )(facts, picks, queries, keys, values, *[array for array, _ in far], *tokens_before)


def gather_kernel(groups, level, part_blocks, facts, picks, source, *outs):
    for turns, out in zip(groups, outs):
        for n, turn in enumerate(turns):
            for i in range(part_blocks):
                block = (facts[0] ^ turn) * part_blocks + i
                out[n * part_blocks + i] = source[picks[block, level]]


def gather(groups, level, part_blocks, facts, picks, source):
    shapes = [(len(turns) * part_blocks,) + source.shape[1:] for turns in groups]
    return pl.pallas_call(
        functools.partial(gather_kernel, groups, level, part_blocks),
        grid_spec=pltpu.PrefetchScalarGridSpec(
            num_scalar_prefetch=2,
            grid=(1,),
            in_specs=[pl.BlockSpec(source.shape, lambda i, f, p: (0, 0, 0, 0))],
            out_specs=[pl.BlockSpec(shape, lambda i, f, p: (0, 0, 0, 0)) for shape in shapes],
        ),
        out_shape=[jax.ShapeDtypeStruct(shape, source.dtype) for shape in shapes],
        compiler_params=pltpu.CompilerParams(vmem_limit_bytes=24 * 2**20),
        cost_estimate=pl.CostEstimate(flops=0, bytes_accessed=2 * 2**20, transcendentals=0),
    )(facts, picks, source)


def after(value, token):
    return lax.optimization_barrier((value, token))[0]


def shards(queries, key_heads, value_tensor, distance_use, block_pick):
    kv_count, tokens, width = key_heads.shape
    levels = distance_use.shape[1]
    ctx_count, head_count = lax.axis_size("ctx"), lax.axis_size("head")
    part = tokens // head_count
    part_blocks = part // BLOCK
    c, j = lax.axis_index("ctx"), lax.axis_index("head")
    live = (distance_use[0] == 1) & (c >= 2 ** jnp.arange(levels))
    queries, keys, shard_values = (
        pltpu.with_memory_space_constraint(a, pltpu.HBM) for a in (queries, key_heads, value_tensor)
    )
    facts = jnp.concatenate([a.astype(jnp.int32) for a in (j[None], live)])
    last = levels - 1

    def forward_pairs(steps):
        return [(s, s + steps) for s in range(ctx_count - steps)]

    def permute(value, pairs):
        return lax.ppermute(value, "ctx", pairs)

    def back(pairs):
        return [(target, source) for source, target in pairs]

    near_pairs = [(s, s + 1) for s in range(0, ctx_count - 1, 2)]
    near_pairs += [(s, s - 1) for s in range(3, ctx_count, 2)]
    far_pairs = forward_pairs(2 ** max(last - 1, 0))

    away, home = list(range(2, head_count)), [1, 0]

    def both(keys, values):
        return jnp.stack([a.reshape(-1, BLOCK, width) for a in (keys, values)], axis=1)

    values = [both(key_heads[0], value_tensor[0])]
    if levels > 2 and kv_count > 1:
        asked = after(block_pick, values[0])
        far_asked = permute(asked, back(far_pairs))
    for kv_index in range(1, kv_count):
        pair = key_heads[kv_index], value_tensor[kv_index]
        values.append(both(*(after(pair, far_asked) if levels > 2 else pair)))

    def short_hops(value, arrived):
        if levels == 1:
            return [(permute(value, forward_pairs(1)), None)]
        source = jnp.where(c % 2 == 0, value, arrived[0])
        return [(permute(source, near_pairs), None)] + [(array, None) for array in arrived]

    def far_hop(value, begin):
        return [(permute(value, far_pairs), begin)] if levels > 2 else []

    def first_hops(value):
        arrived = []
        for level in range(1, max(last, min(levels, 2))):
            steps = 2 ** max(level - 1, 1)
            arrived.append(permute(value if level == 1 else arrived[-1], forward_pairs(steps)))
        return arrived

    def run(far, kv_index, turns, first, before):
        return attend(
            facts, block_pick, queries, keys, shard_values, far, kv_index, turns, first,
            part_blocks, before,
        )

    def send(piece, turn):
        if turn == 0:
            return piece
        return lax.ppermute(piece, "head", [(s, s ^ turn) for s in range(head_count)])

    done, pieces = [], []

    def compute(far, kv_index, turns, first, tokens_before=()):
        out = run(far, kv_index, turns, first, (*done[-1:], *tokens_before))
        done.append(out[0])
        sent = [send(out[i], turn) for i, turn in enumerate(turns)]
        pieces.extend((turn, kv_index, piece) for turn, piece in zip(turns, sent))
        return sent

    heads = [(value, first_hops(value)) for value in values]
    fars, kept, received = [], [], []
    for value, arrived in heads[:-1]:
        far = short_hops(value, arrived)
        sent = [None, None]
        if levels > 2:
            sent = gather([away, home], last, part_blocks, facts, far_asked, arrived[-1])
        fars.append(far + far_hop(sent[0], 0))
        kept.append((far, sent[1]))
    value, arrived = heads[-1]
    fars.append(short_hops(value, arrived) + far_hop(arrived[-1], None))
    final = kv_count - 1
    fars_home = []
    for kv_index in range(final):
        for i, turn in enumerate(away):
            received += compute(fars[kv_index], kv_index, [turn], i)
        far, sent = kept[kv_index]
        fars_home.append(far + far_hop(after(sent, done[0]), 0))
    sent = compute(fars[final], final, away, 0)
    for kv_index in range(final):
        compute(fars_home[kv_index], kv_index, home, 0, received[:1])
    compute(fars[final], final, home[:1], 0)
    compute(fars[final], final, home[1:], 0, (*received[1:], sent[0]))

    out = pl.pallas_call(
        lambda out_ref: None,
        out_specs=pl.BlockSpec(memory_space=pltpu.HBM),
        out_shape=jax.ShapeDtypeStruct(
            (head_count * kv_count, queries.shape[0] // kv_count, part, width), jnp.bfloat16
        ),
    )()
    for turn, kv_index, piece in sorted(pieces, key=lambda p: (p[0] > 1, p[1])):
        place = (j ^ turn) * kv_count + kv_index
        out = lax.dynamic_update_slice_in_dim(out, piece[None], place, 0)
    return out.reshape(-1, part, width)


def solution(mesh):
    placed = (
        P("head", "ctx", None),
        P("head", "ctx", None),
        P("head", "ctx", None),
        P("ctx", None),
        P("ctx", None),
    )
    return jax.shard_map(
        shards,
        mesh=mesh,
        in_specs=placed,
        out_specs=P(None, ("ctx", "head"), None),
        check_vma=False,
    )
```

```python
import functools
import math

import jax
import jax.numpy as jnp
import numpy as np
from jax import lax
from jax.experimental import pallas as pl
from jax.experimental.pallas import tpu as pltpu
from jax.sharding import PartitionSpec as P

BLOCK = 128
MASKED = -1e30


def attend_rows(pairs, block, live, places, group, q_ref, k_ref, v_ref, far, out_ref):
    heads, _, width = q_ref.shape
    rows = group * BLOCK
    coef = math.log2(math.e) / math.sqrt(width)
    near = pairs * 2 * BLOCK
    keys, values = [k_ref[0, :near]], [v_ref[0, :near]]
    for level, place in enumerate(places):
        keys.append(far[level][place, 0])
        values.append(far[level][place, 1])
    keys, values = jnp.concatenate(keys, axis=0), jnp.concatenate(values, axis=0)
    offset = lax.rem(block, 2) * BLOCK
    row = lax.rem(lax.broadcasted_iota(jnp.int32, (rows, 2 * BLOCK), 0), BLOCK)
    col = lax.broadcasted_iota(jnp.int32, (rows, 2 * BLOCK), 1)
    causal = col - row <= offset

    def scores(index):
        q = q_ref[index * group : (index + 1) * group].reshape(rows, width)
        return lax.dot_general(
            q, keys, (((1,), (1,)), ((), ())), preferred_element_type=jnp.float32
        )

    def finish(index, s):
        pieces = []
        if pairs > 1:
            pieces.append(s[:, : near - 2 * BLOCK])
        pieces.append(jnp.where(causal, s[:, near - 2 * BLOCK : near], MASKED))
        for level, used in enumerate(live):
            piece = s[:, near + level * BLOCK : near + (level + 1) * BLOCK]
            pieces.append(jnp.where(used == 1, piece, MASKED))
        s = jnp.concatenate(pieces, axis=1)
        peak = jnp.max(s, axis=1, keepdims=True)
        weights = jnp.exp2((s - peak) * coef)
        total = jnp.sum(weights, axis=1, keepdims=True)
        summed = jnp.dot(weights.astype(jnp.bfloat16), values, preferred_element_type=jnp.float32)
        result = (summed / total).astype(jnp.bfloat16)
        out_ref[index * group : (index + 1) * group] = result.reshape(group, BLOCK, width)

    steps = heads // group
    current = scores(0)
    for index in range(steps):
        following = scores(index + 1) if index + 1 < steps else None
        finish(index, current)
        current = following


def block_at(step, turns, part_blocks, facts):
    turn = turns[-1]
    for n in reversed(range(len(turns) - 1)):
        turn = jnp.where(step // part_blocks == n, turns[n], turn)
    return (facts[0] ^ turn) * part_blocks + lax.rem(step, part_blocks)


def attend_kernel(turns, part_blocks, begins, first, pair_count, facts, picks, *refs):
    q_ref, k_ref, v_ref, out_ref = *refs[:3], refs[-1]
    outs = refs[-1 - len(turns) : -1]
    levels = len(begins)
    far = refs[3 : 3 + levels]
    step = pl.program_id(0)
    block = block_at(step, turns, part_blocks, facts)
    live = [facts[1 + level] for level in range(levels)]
    places = [
        picks[block, level] if begin is None else step + begin + first
        for level, begin in enumerate(begins)
    ]
    for pairs in range(1, pair_count + 1):
        pl.when(block // 2 + 1 == pairs)(
            functools.partial(
                attend_rows, pairs, block, live, places, min(2, q_ref.shape[0]), q_ref, k_ref, v_ref, far, out_ref
            )
        )
    for n, out in enumerate(outs):

        @pl.when(step // part_blocks == n)
        def _(out=out):
            out[...] = out_ref[...]


def attend(facts, picks, queries, keys, values, far, kv_index, turns, first, part_blocks, tokens_before):
    levels = len(far)
    kv_count, tokens, width = keys.shape
    heads = queries.shape[0] // kv_count
    count = len(turns) * part_blocks
    near = pl.BlockSpec((1, tokens, width), lambda i, f, p: (kv_index, 0, 0))

    scores = (tokens // 2 + BLOCK + levels * BLOCK) * count * BLOCK * heads
    return pl.pallas_call(
        functools.partial(
            attend_kernel, turns, part_blocks, [begin for _, begin in far], first * part_blocks,
            tokens // (2 * BLOCK),
        ),
        grid_spec=pltpu.PrefetchScalarGridSpec(
            num_scalar_prefetch=2,
            grid=(count,),
            in_specs=[
                pl.BlockSpec(
                    (heads, BLOCK, width),
                    lambda i, f, p: (kv_index, block_at(i, turns, part_blocks, f), 0),
                ),
                near,
                near,
            ]
            + [pl.BlockSpec(array.shape, lambda i, f, p: (0, 0, 0, 0)) for array, _ in far]
            + [pl.BlockSpec(memory_space=pl.ANY)] * len(tokens_before),
            out_specs=[
                pl.BlockSpec(
                    (heads, BLOCK, width),
                    lambda i, f, p, n=n: (0, jnp.clip(i - n * part_blocks, 0, part_blocks - 1), 0),
                )
                for n in range(len(turns))
            ],
            scratch_shapes=[pltpu.VMEM((heads, BLOCK, width), jnp.bfloat16)],
        ),
        out_shape=[
            jax.ShapeDtypeStruct((heads, part_blocks * BLOCK, width), jnp.bfloat16)
            for _ in turns
        ],
        compiler_params=pltpu.CompilerParams(vmem_limit_bytes=24 * 2**20),
        cost_estimate=pl.CostEstimate(
            flops=24 * scores * width, bytes_accessed=4 * 2**20, transcendentals=scores
        ),
    )(facts, picks, queries, keys, values, *[array for array, _ in far], *tokens_before)


def gather_kernel(groups, level, part_blocks, facts, picks, source, *outs):
    for turns, out in zip(groups, outs):
        for n, turn in enumerate(turns):
            for i in range(part_blocks):
                block = (facts[0] ^ turn) * part_blocks + i
                out[n * part_blocks + i] = source[picks[block, level]]


def gather(groups, level, part_blocks, facts, picks, source):
    shapes = [(len(turns) * part_blocks,) + source.shape[1:] for turns in groups]
    return pl.pallas_call(
        functools.partial(gather_kernel, groups, level, part_blocks),
        grid_spec=pltpu.PrefetchScalarGridSpec(
            num_scalar_prefetch=2,
            grid=(1,),
            in_specs=[pl.BlockSpec(source.shape, lambda i, f, p: (0, 0, 0, 0))],
            out_specs=[pl.BlockSpec(shape, lambda i, f, p: (0, 0, 0, 0)) for shape in shapes],
        ),
        out_shape=[jax.ShapeDtypeStruct(shape, source.dtype) for shape in shapes],
        compiler_params=pltpu.CompilerParams(vmem_limit_bytes=24 * 2**20),
        cost_estimate=pl.CostEstimate(flops=0, bytes_accessed=2 * 2**20, transcendentals=0),
    )(facts, picks, source)


def after(value, token):
    return lax.optimization_barrier((value, token))[0]


def shards(queries, key_heads, value_tensor, distance_use, block_pick):
    kv_count, tokens, width = key_heads.shape
    levels = distance_use.shape[1]
    ctx_count, head_count = lax.axis_size("ctx"), lax.axis_size("head")
    part = tokens // head_count
    part_blocks = part // BLOCK
    c, j = lax.axis_index("ctx"), lax.axis_index("head")
    live = (distance_use[0] == 1) & (c >= 2 ** jnp.arange(levels))
    queries, keys, shard_values = (
        pltpu.with_memory_space_constraint(a, pltpu.HBM) for a in (queries, key_heads, value_tensor)
    )
    facts = jnp.concatenate([a.astype(jnp.int32) for a in (j[None], live)])
    last = levels - 1

    def forward_pairs(steps):
        return [(s, s + steps) for s in range(ctx_count - steps)]

    def permute(value, pairs):
        return lax.ppermute(value, "ctx", pairs)

    def back(pairs):
        return [(target, source) for source, target in pairs]

    near_pairs = [(s, s + 1) for s in range(0, ctx_count - 1, 2)]
    near_pairs += [(s, s - 1) for s in range(3, ctx_count, 2)]
    far_pairs = forward_pairs(2 ** max(last - 1, 0))

    away, home = list(range(2, head_count)), [1, 0]

    def both(keys, values):
        return jnp.stack([a.reshape(-1, BLOCK, width) for a in (keys, values)], axis=1)

    values = [both(key_heads[0], value_tensor[0])]
    if levels > 2 and kv_count > 1:
        asked = after(block_pick, values[0])
        far_asked = permute(asked, back(far_pairs))
    for kv_index in range(1, kv_count):
        pair = key_heads[kv_index], value_tensor[kv_index]
        values.append(both(*(after(pair, far_asked) if levels > 2 else pair)))

    def short_hops(value, arrived):
        if levels == 1:
            return [(permute(value, forward_pairs(1)), None)]
        source = jnp.where(c % 2 == 0, value, arrived[0])
        return [(permute(source, near_pairs), None)] + [(array, None) for array in arrived]

    def far_hop(value, begin):
        return [(permute(value, far_pairs), begin)] if levels > 2 else []

    def first_hops(value):
        arrived = []
        for level in range(1, max(last, min(levels, 2))):
            steps = 2 ** max(level - 1, 1)
            arrived.append(permute(value if level == 1 else arrived[-1], forward_pairs(steps)))
        return arrived

    def run(far, kv_index, turns, first, before):
        return attend(
            facts, block_pick, queries, keys, shard_values, far, kv_index, turns, first,
            part_blocks, before,
        )

    def send(piece, turn):
        if turn == 0:
            return piece
        return lax.ppermute(piece, "head", [(s, s ^ turn) for s in range(head_count)])

    done, pieces = [], []

    def compute(far, kv_index, turns, first, tokens_before=()):
        out = run(far, kv_index, turns, first, (*done[-1:], *tokens_before))
        done.append(out[0])
        sent = [send(out[i], turn) for i, turn in enumerate(turns)]
        pieces.extend((turn, kv_index, piece) for turn, piece in zip(turns, sent))
        return sent

    heads = [(value, first_hops(value)) for value in values]
    fars, fars_home, received = [], [], []
    for value, arrived in heads[:-1]:
        far = short_hops(value, arrived)
        sent = [None, None]
        if levels > 2:
            sent = gather([away, home], last, part_blocks, facts, far_asked, arrived[-1])
        fars.append(far + far_hop(sent[0], 0))
        fars_home.append(far + far_hop(sent[1], 0))
    value, arrived = heads[-1]
    fars.append(short_hops(value, arrived) + far_hop(arrived[-1], None))
    final = kv_count - 1
    for kv_index in range(final):
        for i, turn in enumerate(away):
            received += compute(fars[kv_index], kv_index, [turn], i)
    sent = compute(fars[final], final, away, 0)
    for kv_index in range(final):
        compute(fars_home[kv_index], kv_index, home, 0, received[:1])
    compute(fars[final], final, home[:1], 0)
    compute(fars[final], final, home[1:], 0, (*received[1:], sent[0]))

    out = pl.pallas_call(
        lambda out_ref: None,
        out_specs=pl.BlockSpec(memory_space=pltpu.HBM),
        out_shape=jax.ShapeDtypeStruct(
            (head_count * kv_count, queries.shape[0] // kv_count, part, width), jnp.bfloat16
        ),
    )()
    for turn, kv_index, piece in sorted(pieces, key=lambda p: (p[0] > 1, p[1])):
        place = (j ^ turn) * kv_count + kv_index
        out = lax.dynamic_update_slice_in_dim(out, piece[None], place, 0)
    return out.reshape(-1, part, width)


def solution(mesh):
    placed = (
        P("head", "ctx", None),
        P("head", "ctx", None),
        P("head", "ctx", None),
        P("ctx", None),
        P("ctx", None),
    )
    return jax.shard_map(
        shards,
        mesh=mesh,
        in_specs=placed,
        out_specs=P(None, ("ctx", "head"), None),
        check_vma=False,
    )
```

```python
import functools
import math

import jax
import jax.numpy as jnp
import numpy as np
from jax import lax
from jax.experimental import pallas as pl
from jax.experimental.pallas import tpu as pltpu
from jax.sharding import PartitionSpec as P

BLOCK = 128
MASKED = -1e30


def attend_rows(pairs, block, live, group, q_ref, k_ref, v_ref, far, out_ref):
    heads, _, width = q_ref.shape
    rows = group * BLOCK
    coef = math.log2(math.e) / math.sqrt(width)
    near = pairs * 2 * BLOCK
    keys, values = [k_ref[0, :near]], [v_ref[0, :near]]
    for array in far:
        keys.append(array[0, 0])
        values.append(array[0, 1])
    keys, values = jnp.concatenate(keys, axis=0), jnp.concatenate(values, axis=0)
    offset = lax.rem(block, 2) * BLOCK
    row = lax.rem(lax.broadcasted_iota(jnp.int32, (rows, 2 * BLOCK), 0), BLOCK)
    col = lax.broadcasted_iota(jnp.int32, (rows, 2 * BLOCK), 1)
    causal = col - row <= offset

    def scores(index):
        q = q_ref[index * group : (index + 1) * group].reshape(rows, width)
        return lax.dot_general(
            q, keys, (((1,), (1,)), ((), ())), preferred_element_type=jnp.float32
        )

    def finish(index, s):
        pieces = []
        if pairs > 1:
            pieces.append(s[:, : near - 2 * BLOCK])
        pieces.append(jnp.where(causal, s[:, near - 2 * BLOCK : near], MASKED))
        for level, used in enumerate(live):
            piece = s[:, near + level * BLOCK : near + (level + 1) * BLOCK]
            pieces.append(jnp.where(used == 1, piece, MASKED))
        s = jnp.concatenate(pieces, axis=1)
        peak = jnp.max(s, axis=1, keepdims=True)
        weights = jnp.exp2((s - peak) * coef)
        total = jnp.sum(weights, axis=1, keepdims=True)
        summed = jnp.dot(weights.astype(jnp.bfloat16), values, preferred_element_type=jnp.float32)
        result = (summed / total).astype(jnp.bfloat16)
        out_ref[index * group : (index + 1) * group] = result.reshape(group, BLOCK, width)

    steps = heads // group
    current = scores(0)
    for index in range(steps):
        following = scores(index + 1) if index + 1 < steps else None
        finish(index, current)
        current = following


def block_at(step, turns, part_blocks, facts):
    turn = turns[-1]
    for n in reversed(range(len(turns) - 1)):
        turn = jnp.where(step // part_blocks == n, turns[n], turn)
    return (facts[0] ^ turn) * part_blocks + lax.rem(step, part_blocks)


def attend_kernel(turns, part_blocks, levels, pair_count, facts, picks, *refs):
    q_ref, k_ref, v_ref, out_ref = *refs[:3], refs[-1]
    outs = refs[-1 - len(turns) : -1]
    if len(turns) == 1:
        out_ref, outs = outs[0], []
    far = refs[3 : 3 + levels]
    step = pl.program_id(0)
    block = block_at(step, turns, part_blocks, facts)
    live = [facts[1 + level] for level in range(levels)]
    for pairs in range(1, pair_count + 1):
        pl.when(block // 2 + 1 == pairs)(
            functools.partial(
                attend_rows, pairs, block, live, min(2, q_ref.shape[0]), q_ref, k_ref, v_ref, far, out_ref
            )
        )
    for n, out in enumerate(outs):

        @pl.when(step // part_blocks == n)
        def _(out=out):
            out[...] = out_ref[...]


def attend(facts, picks, queries, keys, values, far, kv_index, turns, first, part_blocks, tokens_before):
    levels = len(far)
    kv_count, tokens, width = keys.shape
    heads = queries.shape[0] // kv_count
    count = len(turns) * part_blocks
    near = pl.BlockSpec((1, tokens, width), lambda i, f, p: (kv_index, 0, 0))

    def picked(level, begin):
        def place(i, f, p):
            if begin is None:
                return p[block_at(i, turns, part_blocks, f), level], 0, 0, 0
            return i + begin + first * part_blocks, 0, 0, 0

        return pl.BlockSpec((1, 2, BLOCK, width), place)

    scores = (tokens // 2 + BLOCK + levels * BLOCK) * count * BLOCK * heads
    return pl.pallas_call(
        functools.partial(attend_kernel, turns, part_blocks, levels, tokens // (2 * BLOCK)),
        grid_spec=pltpu.PrefetchScalarGridSpec(
            num_scalar_prefetch=2,
            grid=(count,),
            in_specs=[
                pl.BlockSpec(
                    (heads, BLOCK, width),
                    lambda i, f, p: (kv_index, block_at(i, turns, part_blocks, f), 0),
                ),
                near,
                near,
            ]
            + [picked(level, begin) for level, (_, begin) in enumerate(far)]
            + [pl.BlockSpec(memory_space=pl.ANY)] * len(tokens_before),
            out_specs=[
                pl.BlockSpec(
                    (heads, BLOCK, width),
                    lambda i, f, p, n=n: (0, jnp.clip(i - n * part_blocks, 0, part_blocks - 1), 0),
                )
                for n in range(len(turns))
            ],
            scratch_shapes=[pltpu.VMEM((heads, BLOCK, width), jnp.bfloat16)],
        ),
        out_shape=[
            jax.ShapeDtypeStruct((heads, part_blocks * BLOCK, width), jnp.bfloat16)
            for _ in turns
        ],
        compiler_params=pltpu.CompilerParams(vmem_limit_bytes=24 * 2**20),
        cost_estimate=pl.CostEstimate(
            flops=24 * scores * width, bytes_accessed=4 * 2**20, transcendentals=scores
        ),
    )(facts, picks, queries, keys, values, *[array for array, _ in far], *tokens_before)


def gather_kernel(groups, level, part_blocks, facts, picks, source, *outs):
    for turns, out in zip(groups, outs):
        for n, turn in enumerate(turns):
            for i in range(part_blocks):
                block = (facts[0] ^ turn) * part_blocks + i
                out[n * part_blocks + i] = source[picks[block, level]]


def gather(groups, level, part_blocks, facts, picks, source):
    shapes = [(len(turns) * part_blocks,) + source.shape[1:] for turns in groups]
    return pl.pallas_call(
        functools.partial(gather_kernel, groups, level, part_blocks),
        grid_spec=pltpu.PrefetchScalarGridSpec(
            num_scalar_prefetch=2,
            grid=(1,),
            in_specs=[pl.BlockSpec(source.shape, lambda i, f, p: (0, 0, 0, 0))],
            out_specs=[pl.BlockSpec(shape, lambda i, f, p: (0, 0, 0, 0)) for shape in shapes],
        ),
        out_shape=[jax.ShapeDtypeStruct(shape, source.dtype) for shape in shapes],
        compiler_params=pltpu.CompilerParams(vmem_limit_bytes=24 * 2**20),
        cost_estimate=pl.CostEstimate(flops=0, bytes_accessed=2 * 2**20, transcendentals=0),
    )(facts, picks, source)


def after(value, token):
    return lax.optimization_barrier((value, token))[0]


def shards(queries, key_heads, value_tensor, distance_use, block_pick):
    kv_count, tokens, width = key_heads.shape
    levels = distance_use.shape[1]
    ctx_count, head_count = lax.axis_size("ctx"), lax.axis_size("head")
    part = tokens // head_count
    part_blocks = part // BLOCK
    c, j = lax.axis_index("ctx"), lax.axis_index("head")
    live = (distance_use[0] == 1) & (c >= 2 ** jnp.arange(levels))
    queries, keys, shard_values = (
        pltpu.with_memory_space_constraint(a, pltpu.HBM) for a in (queries, key_heads, value_tensor)
    )
    facts = jnp.concatenate([a.astype(jnp.int32) for a in (j[None], live)])
    last = levels - 1

    def forward_pairs(steps):
        return [(s, s + steps) for s in range(ctx_count - steps)]

    def permute(value, pairs):
        return lax.ppermute(value, "ctx", pairs)

    def back(pairs):
        return [(target, source) for source, target in pairs]

    near_pairs = [(s, s + 1) for s in range(0, ctx_count - 1, 2)]
    near_pairs += [(s, s - 1) for s in range(3, ctx_count, 2)]
    far_pairs = forward_pairs(2 ** max(last - 1, 0))

    away, home = list(range(2, head_count)), [1, 0]

    def both(keys, values):
        return jnp.stack([a.reshape(-1, BLOCK, width) for a in (keys, values)], axis=1)

    values = [both(key_heads[0], value_tensor[0])]
    if levels > 2 and kv_count > 1:
        asked = after(block_pick, values[0])
        far_asked = permute(asked, back(far_pairs))
    for kv_index in range(1, kv_count):
        pair = key_heads[kv_index], value_tensor[kv_index]
        values.append(both(*(after(pair, far_asked) if levels > 2 else pair)))

    def short_hops(value, arrived):
        if levels == 1:
            return [(permute(value, forward_pairs(1)), None)]
        source = jnp.where(c % 2 == 0, value, arrived[0])
        return [(permute(source, near_pairs), None)] + [(array, None) for array in arrived]

    def far_hop(value, begin):
        return [(permute(value, far_pairs), begin)] if levels > 2 else []

    def first_hops(value):
        arrived = []
        for level in range(1, max(last, min(levels, 2))):
            steps = 2 ** max(level - 1, 1)
            arrived.append(permute(value if level == 1 else arrived[-1], forward_pairs(steps)))
        return arrived

    def run(far, kv_index, turns, first, before):
        return attend(
            facts, block_pick, queries, keys, shard_values, far, kv_index, turns, first,
            part_blocks, before,
        )

    def send(piece, turn):
        if turn == 0:
            return piece
        return lax.ppermute(piece, "head", [(s, s ^ turn) for s in range(head_count)])

    done, pieces = [], []

    def compute(far, kv_index, turns, first, tokens_before=()):
        out = run(far, kv_index, turns, first, (*done[-1:], *tokens_before))
        done.append(out[0])
        sent = [send(out[i], turn) for i, turn in enumerate(turns)]
        pieces.extend((turn, kv_index, piece) for turn, piece in zip(turns, sent))
        return sent

    heads = [(value, first_hops(value)) for value in values]
    fars, fars_home, received = [], [], []
    for value, arrived in heads[:-1]:
        far = short_hops(value, arrived)
        sent = [None, None]
        if levels > 2:
            sent = gather([away, home], last, part_blocks, facts, far_asked, arrived[-1])
        fars.append(far + far_hop(sent[0], 0))
        fars_home.append(far + far_hop(sent[1], 0))
    value, arrived = heads[-1]
    fars.append(short_hops(value, arrived) + far_hop(arrived[-1], None))
    final = kv_count - 1
    for kv_index in range(final):
        for i, turn in enumerate(away):
            received += compute(fars[kv_index], kv_index, [turn], i)
    sent = compute(fars[final], final, away, 0)
    for kv_index in range(final):
        compute(fars_home[kv_index], kv_index, home, 0, received[:1])
    compute(fars[final], final, home[:1], 0)
    compute(fars[final], final, home[1:], 0, (*received[1:], sent[0]))

    out = pl.pallas_call(
        lambda out_ref: None,
        out_specs=pl.BlockSpec(memory_space=pltpu.HBM),
        out_shape=jax.ShapeDtypeStruct(
            (head_count * kv_count, queries.shape[0] // kv_count, part, width), jnp.bfloat16
        ),
    )()
    for turn, kv_index, piece in sorted(pieces, key=lambda p: (p[0] > 1, p[1])):
        place = (j ^ turn) * kv_count + kv_index
        out = lax.dynamic_update_slice_in_dim(out, piece[None], place, 0)
    return out.reshape(-1, part, width)


def solution(mesh):
    placed = (
        P("head", "ctx", None),
        P("head", "ctx", None),
        P("head", "ctx", None),
        P("ctx", None),
        P("ctx", None),
    )
    return jax.shard_map(
        shards,
        mesh=mesh,
        in_specs=placed,
        out_specs=P(None, ("ctx", "head"), None),
        check_vma=False,
    )
```
